512 devices in a mesh: grp: 8 (over x, y_hi), lon: 16 (over z), lat: 4 (over y_lo, core).
Axes of the slice: x: 4, y: 4 (y_hi: 2, y_lo: 2; y = y_hi * 2 + y_lo), z: 16, core: 2. Of those that a mesh axis runs over, the one named last changes fastest.
Arguments:
- tracers: float32 [64, 256, 64, 128], P('grp', 'lon', 'lat'), may hold values from -6 to 6
- fluxes: float32 [2, 3, 256, 64, 128], P(None, None, 'lon', 'lat', 'grp'), may hold values from -0.3 to 0.3
- limiter_mask: int32 [2, 256, 64, 128], P(None, 'lon', 'lat'), may hold values 0 or 1
- diffusion_inverse: float32 [2, 64, 128, 128], P(None, 'lat'), may hold values from 0 to 1, as said below
Outputs:
- transported: float32 [64, 256, 64, 128], P('grp', 'lon', 'lat')
The draws below stay inside these ranges and needn't reach their ends.
Inputs may be any that keep to these rules, and one draw needn't show every extreme that they name: diffusion_inverse[s, j] is symmetric with positive entries and is the inverse of a symmetric tridiagonal matrix.
All inputs are finite; a program needn't handle non-finite values. No bound on the sum of `limiter_mask` on one device may be relied on, other than what follows from the above.
Results may differ from the reference program's by a relative error of at most 0.0001.
Values sent between devices are 32-bit elements; how exact they have to be, the bound alone decides.
A program may use at most 64 MiB of HBM per device.

```python
import math
import jax
import jax.numpy as jnp
from jax import lax

NZ = 128
STEPS = 2
NX = 256
NY = 64
TRACERS = 64


def draw_diffusion_inverse(key, part):
    key = jax.random.fold_in(key, 11)
    key_pos, key_len, key_gain = jax.random.split(key, 3)
    jitter = jax.random.uniform(key_pos, (STEPS, NY, NZ), jnp.float32, 0.0, 1.0)
    heights = jnp.arange(NZ).astype(jnp.float32)[None, None, :] + 0.45 * jitter
    length = jnp.exp(jax.random.uniform(key_len, (STEPS, NY, 1, 1), jnp.float32, math.log(1.5), math.log(6.0)))
    gains = jax.random.uniform(key_gain, (STEPS, NY, NZ), jnp.float32, 0.6, 1.0)
    distance = jnp.abs(heights[..., :, None] - heights[..., None, :])
    kernel = jnp.exp(-distance / length) / (1.0 + 2.0 * length)
    return (gains[..., :, None] * gains[..., None, :] * kernel).astype(jnp.float32)


def touch_ends(drawn, own_key, low, high):
    spot = [jax.random.randint(jax.random.fold_in(own_key, axis), (), 0, length) for axis, length in enumerate(drawn.shape)]
    longest = drawn.shape.index(max(drawn.shape))
    next_to = spot[:longest] + [(spot[longest] + 1) % drawn.shape[longest]] + spot[longest + 1:]
    return drawn.at[tuple(spot)].set(low).at[tuple(next_to)].set(high)


def steps_of(own_key, extent, shards, low, largest):
    factor_of = 1.0
    for axis_at, blocks in shards:
        draws = jax.random.uniform(jax.random.fold_in(jax.random.fold_in(own_key, 6), axis_at), (blocks,), jnp.float32, low / len(shards), largest / len(shards))
        factor_of = factor_of * jnp.repeat(jnp.exp(draws), extent[axis_at] // blocks).reshape((-1,) + (1,) * (len(extent) - 1 - axis_at))
    return factor_of


def scatter_about(own_key, shape, scale, bound, shards=(), held_as=jnp.bfloat16):
    factor_of = steps_of(own_key, shape, shards, -0.22, 0.18) if shards else 1.0
    drawn = jax.random.normal(own_key, shape, jnp.float32) * scale * factor_of
    return jnp.minimum(jnp.maximum(drawn, -bound), bound).astype(held_as)


def setup_inputs(seed: int = 0) -> dict:
    arg_keys = jax.random.split(jax.random.key(seed), 5)
    tracers = scatter_about(arg_keys[0], (TRACERS, NX, NY, NZ), 1.0, 6.0, ((0, 8), (1, 16), (2, 4)), jnp.float32)
    fluxes = jnp.clip(jax.random.uniform(arg_keys[1], (STEPS, 3, NX, NY, NZ), jnp.float32, -0.3, 0.3) * steps_of(arg_keys[1], (STEPS, 3, NX, NY, NZ), ((2, 16), (3, 4), (4, 8)), -0.4, 0.0), -0.3, 0.3)
    limiter_mask = touch_ends((jax.random.randint(arg_keys[2], (STEPS, NX, NY, NZ), 0, 4) < 1).astype(jnp.int32), jax.random.fold_in(arg_keys[2], 1), 0, 1)
    diffusion_inverse = draw_diffusion_inverse(jax.random.fold_in(arg_keys[4], 71), 0)
    return {"tracers": tracers, "fluxes": fluxes, "limiter_mask": limiter_mask, "diffusion_inverse": diffusion_inverse}


def third_order(minus_two, minus_one, plus_zero, plus_one, courant):
    return courant * (7.0 * (plus_zero + minus_one) - (plus_one + minus_two)) / 12.0 + jnp.abs(courant) * ((plus_one - minus_two) - 3.0 * (plus_zero - minus_one)) / 12.0


def first_order(minus_one, plus_zero, courant):
    return courant * (plus_zero + minus_one) / 2.0 - jnp.abs(courant) * (plus_zero - minus_one) / 2.0


def vertical_change(values, courant, limiter):
    depth = values.shape[-1]
    padded = jnp.pad(values, [(0, 0)] * (values.ndim - 1) + [(2, 2)])
    high = third_order(padded[..., 0:depth], padded[..., 1:depth + 1], padded[..., 2:depth + 2], padded[..., 3:depth + 3], courant)
    low = first_order(padded[..., 1:depth + 1], padded[..., 2:depth + 2], courant)
    level_idx = jnp.arange(depth)
    faces = jnp.where(level_idx == 0, 0.0, jnp.where((level_idx == 1) | (level_idx == depth - 1) | (limiter == 1), low, high))
    following = jnp.concatenate([faces[..., 1:], jnp.zeros_like(faces[..., :1])], axis=-1)
    return faces - following


def advect_whole(values, courants, limiter):
    eastward = courants[0]
    northward = courants[1]
    upward = courants[2]
    lon_faces = third_order(jnp.roll(values, 2, 0), jnp.roll(values, 1, 0), values, jnp.roll(values, -1, 0), eastward)
    change_lon = lon_faces - jnp.roll(lon_faces, -1, 0)
    row_total = values.shape[1]
    padded = jnp.pad(values, ((0, 0), (2, 2), (0, 0)))
    high = third_order(padded[:, 0:row_total], padded[:, 1:row_total + 1], padded[:, 2:row_total + 2], padded[:, 3:row_total + 3], northward)
    low = first_order(padded[:, 1:row_total + 1], padded[:, 2:row_total + 2], northward)
    row_idx = jnp.arange(row_total)[None, :, None]
    lat_faces = jnp.where(row_idx == 0, 0.0, jnp.where((row_idx == 1) | (row_idx == row_total - 1), low, high))
    following = jnp.concatenate([lat_faces[:, 1:], jnp.zeros_like(lat_faces[:, :1])], axis=1)
    change_lat = lat_faces - following
    return values + change_lon + change_lat + vertical_change(values, upward, limiter)


def reference(tracers, fluxes, limiter_mask, diffusion_inverse):
    def one_tracer(values):
        for step_no in range(STEPS):
            values = advect_whole(values, fluxes[step_no], limiter_mask[step_no])
            values = jnp.einsum("jzk,ijk->ijz", diffusion_inverse[step_no], values, precision=lax.Precision.HIGHEST)
        return values
    return lax.map(one_tracer, tracers)
```

```python
import functools

import jax
import jax.numpy as jnp
from jax import lax
from jax.experimental import pallas as pl
from jax.experimental.pallas import tpu as pltpu
from jax.sharding import PartitionSpec as P

MESH = pl.DeviceIdType.MESH
LANES = 128
POINTS = 13


def faces(courant, first=None):
    plus, minus = jnp.maximum(courant, 0.0), jnp.minimum(courant, 0.0)
    p, m = plus * (1.0 / 6.0), minus * (1.0 / 6.0)
    a, b, c, d = -p, 5.0 * p + 2.0 * m, 2.0 * p + 5.0 * m, -m
    if first is not None:
        a, b = jnp.where(first, 0.0, a), jnp.where(first, plus, b)
        c, d = jnp.where(first, minus, c), jnp.where(first, 0.0, d)
    return a, b, c, d


def spread(low, high):
    a, b, c, d = low
    e, f, g, h = high
    return a, b - e, c - f, d - g, -h


def block_transpose(blocks, lane):
    blocks = list(blocks)
    for bit in (1, 2, 4):
        odd = (lane // (16 * bit)) % 2 == 1
        for g in range(8):
            if g & bit:
                continue
            low, high = blocks[g], blocks[g + bit]
            blocks[g] = jnp.where(odd, pltpu.roll(high, 16 * bit, 1), low)
            blocks[g + bit] = jnp.where(odd, high, pltpu.roll(low, LANES - 16 * bit, 1))
    return blocks


def kernel(
    tracers, fluxes, limiter, inverse, out,
    shard, gath, near, ext, start, field, given, weights, coef, courant, lim, split, done,
    in_sem, out_sem, near_send, near_recv, ext_send, ext_recv, gath_send, gath_recv,
    halo_send, halo_recv, lon_send, lon_recv, lat_send, lat_recv,
):
    groups, lons, lats = lax.axis_size("grp"), lax.axis_size("lon"), lax.axis_size("lat")
    grp, lon, lat = lax.axis_index("grp"), lax.axis_index("lon"), lax.axis_index("lat")
    east, west = lax.rem(lon + 1, lons), lax.rem(lon + lons - 1, lons)
    has_south, has_north = lat > 0, lat < lats - 1
    south, north = lat - 1, lat + 1
    peers = [lax.rem(grp + d, groups) for d in range(1, groups)]
    lane = lax.broadcasted_iota(jnp.int32, (8, LANES), 1)
    sub = lax.broadcasted_iota(jnp.int32, (8, LANES), 0)

    def remote(src, dst, send, recv, where):
        return pltpu.make_async_remote_copy(
            src_ref=src, dst_ref=dst, send_sem=send, recv_sem=recv,
            device_id=where, device_id_type=MESH,
        )

    loads = [
        pltpu.make_async_copy(fluxes.at[0], shard.at[0], in_sem.at[0]),
        pltpu.make_async_copy(tracers, start, in_sem.at[1]),
        pltpu.make_async_copy(fluxes.at[1], shard.at[1], in_sem.at[2]),
        pltpu.make_async_copy(limiter, lim, in_sem.at[3]),
        pltpu.make_async_copy(inverse, given, in_sem.at[4]),
    ]
    for load in loads:
        load.start()

    barrier = pltpu.get_barrier_semaphore()
    for peer in peers:
        pl.semaphore_signal(barrier, inc=1, device_id={"grp": peer}, device_id_type=MESH)
    for side in (east, west):
        pl.semaphore_signal(barrier, inc=1, device_id={"lon": side}, device_id_type=MESH)

    @pl.when(has_south)
    def _():
        pl.semaphore_signal(barrier, inc=1, device_id={"lat": south}, device_id_type=MESH)

    @pl.when(has_north)
    def _():
        pl.semaphore_signal(barrier, inc=1, device_id={"lat": north}, device_id_type=MESH)

    def pack(step):
        def body(q, _):
            base = pl.multiple_of((q // 4) * 256 + ((q // 2) % 2) * 128 + (q % 2) * 8, 8)
            parts = [shard[step, pl.ds(base + 16 * r, 8), :] for r in range(8)]
            gath[step, grp, pl.ds(pl.multiple_of(q * 8, 8), 8), :] = jnp.concatenate(parts, axis=1)
            return 0

        lax.fori_loop(0, 12, body, 0)

    def send_gath(step):
        for d, peer in enumerate(peers):
            remote(
                gath.at[step, grp], gath.at[step, grp],
                gath_send.at[step, d], gath_recv.at[step, d], {"grp": peer},
            ).start()

    loads[0].wait()
    pack(0)
    loads[2].wait()
    cols = [shard[s, pl.ds(8 * jb, 8), :] for s in range(2) for jb in range(2)]
    rows = [shard[s, pl.ds(256 + 128 * ib, 8, stride=16), :] for s in range(2) for ib in range(2)]
    near[0] = jnp.concatenate(cols + rows, axis=1)

    pl.semaphore_wait(barrier, groups + 1 + jnp.minimum(lat, 1) + jnp.minimum(lats - 1 - lat, 1))

    to_west = remote(near.at[0], near.at[1], near_send.at[0], near_recv.at[0], {"lon": west})
    to_south = remote(near.at[0], near.at[2], near_send.at[1], near_recv.at[1], {"lat": south})
    to_west.start()

    @pl.when(has_south)
    def _():
        to_south.start()

    send_gath(0)

    loads[1].wait()

    def turn(j, _):
        for i in range(16):
            field[0, j + 2, i + 2] = start[pl.ds(i * 16 + j, 8, stride=256), :]
        return 0

    lax.fori_loop(0, 16, turn, 0)

    for s in range(2):
        @pl.when(jnp.logical_not(has_south))
        def _():
            field[s, 0:2] = jnp.zeros((2, 20, 8, LANES), jnp.float32)

        @pl.when(jnp.logical_not(has_north))
        def _():
            field[s, 18:20] = jnp.zeros((2, 20, 8, LANES), jnp.float32)

    halo_west = remote(
        field.at[0, pl.ds(2, 16), pl.ds(2, 2)], field.at[0, pl.ds(2, 16), pl.ds(18, 2)],
        halo_send.at[0], halo_recv.at[0], {"lon": west},
    )
    halo_east = remote(
        field.at[0, pl.ds(2, 16), pl.ds(16, 2)], field.at[0, pl.ds(2, 16), pl.ds(0, 2)],
        halo_send.at[1], halo_recv.at[1], {"lon": east},
    )

    def lat_copies(step, send, recv):
        to_s = remote(
            field.at[step, pl.ds(2, 2), pl.ds(2, 16)], field.at[step, pl.ds(18, 2), pl.ds(2, 16)],
            send.at[0], recv.at[0], {"lat": south},
        )
        to_n = remote(
            field.at[step, pl.ds(16, 2), pl.ds(2, 16)], field.at[step, pl.ds(0, 2), pl.ds(2, 16)],
            send.at[1], recv.at[1], {"lat": north},
        )
        return to_s, to_n

    halo_south, halo_north = lat_copies(0, halo_send.at[pl.ds(2, 2)], halo_recv.at[pl.ds(2, 2)])
    halo_west.start()
    halo_east.start()

    @pl.when(has_south)
    def _():
        halo_south.start()

    @pl.when(has_north)
    def _():
        halo_north.start()

    to_west.wait_recv()

    @pl.when(has_north)
    def _():
        to_south.wait_recv()
        ext[grp] = jnp.where(lane < 64, near[1], near[2])

    @pl.when(jnp.logical_not(has_north))
    def _():
        ext[grp] = jnp.where(lane < 64, near[1], 0.0)

    for d, peer in enumerate(peers):
        remote(ext.at[grp], ext.at[grp], ext_send.at[d], ext_recv.at[d], {"grp": peer}).start()

    pack(1)
    send_gath(1)

    loads[4].wait()
    for s in range(2):
        def halve(j, _):
            full = given[s, j]
            high = full.astype(jnp.bfloat16)
            low = (full - high.astype(jnp.float32)).astype(jnp.bfloat16)
            for top in (0, 128):
                weights[s, j, top:top + 128, 0:128] = high
                weights[s, j, top:top + 128, 128:256] = low
            return 0

        lax.fori_loop(0, 16, halve, 0)

    loads[3].wait()
    first_row = lat * 16
    last_row = lats * 16

    def prepare(step):
        def unpack(q, _):
            rows = pl.ds(pl.multiple_of(q * 8, 8), 8)
            full = block_transpose([gath[step, g, rows, :] for g in range(8)], lane)
            at = pl.multiple_of((q % 2) * 8, 8)
            for r in range(8):
                courant[q // 4, ((q // 2) % 2) * 8 + r, pl.ds(at, 8), :] = full[r]
            return 0

        lax.fori_loop(0, 12, unpack, 0)
        edges = block_transpose([ext[g] for g in range(8)], lane)
        for jb in range(2):
            courant[0, 16, 8 * jb:8 * jb + 8, :] = edges[2 * step + jb]
        for ib in range(2):
            values = edges[4 + 2 * step + ib]
            for r in range(8):
                courant[1, 8 * ib + r, 16:17, :] = values[r:r + 1]

        def column(i, _):
            for jb in range(2):
                here = pl.ds(8 * jb, 8)
                w2, w1, lon0, e1, e2 = spread(faces(courant[0, i, here, :]), faces(courant[0, i + 1, here, :]))
                row = first_row + 8 * jb + sub

                def lat_faces(v, face_row):
                    v = jnp.where((face_row == 0) | (face_row == last_row), 0.0, v)
                    return faces(v, (face_row == 1) | (face_row == last_row - 1))

                s2, s1, lat0, n1, n2 = spread(
                    lat_faces(courant[1, i, here, :], row),
                    lat_faces(courant[1, i, pl.ds(8 * jb + 1, 8), :], row + 1),
                )
                up = jnp.where(lane == 0, 0.0, courant[2, i, here, :])
                low = faces(up, (lane == 1) | (lane == LANES - 1) | (lim[step, i, here, :] == 1))
                high = [pltpu.roll(x, LANES - 1, 1) for x in low]
                d2, d1, ver0, u1, u2 = spread(low, high)
                every = (1.0 + lon0 + lat0 + ver0, w2, w1, e1, e2, s2, s1, n1, n2, d2, d1, u1, u2)
                for n, value in enumerate(every):
                    coef[n, i, here, :] = value
            return 0

        lax.fori_loop(0, 16, column, 0)

    def advance(step, j, write):
        mid = [field[step, j + 2, i] for i in range(20)]
        for pair in range(8):
            new = []
            for i in (2 * pair, 2 * pair + 1):
                c = [jnp.broadcast_to(coef[n, i, pl.ds(j, 1), :], (8, LANES)) for n in range(POINTS)]
                q = mid[i + 2]
                lon_part = c[1] * mid[i] + c[2] * mid[i + 1] + c[3] * mid[i + 3] + c[4] * mid[i + 4]
                lat_part = (
                    c[5] * field[step, j, i + 2] + c[6] * field[step, j + 1, i + 2]
                    + c[7] * field[step, j + 3, i + 2] + c[8] * field[step, j + 4, i + 2]
                )
                ver_part = (
                    c[9] * pltpu.roll(q, 2, 1) + c[10] * pltpu.roll(q, 1, 1)
                    + c[11] * pltpu.roll(q, LANES - 1, 1) + c[12] * pltpu.roll(q, LANES - 2, 1)
                )
                new.append(c[0] * q + lon_part + (lat_part + ver_part))
            both = jnp.concatenate(new, axis=0)
            high = both.astype(jnp.bfloat16)
            split[16 * pair:16 * pair + 16, 0:128] = high
            split[16 * pair:16 * pair + 16, 128:256] = (both - high.astype(jnp.float32)).astype(jnp.bfloat16)
        product = jnp.dot(split[...], weights[step, j], preferred_element_type=jnp.float32)
        total = product[:, 0:128] + product[:, 128:256]
        for i in range(16):
            write(j, i, total[8 * i:8 * i + 8])

    for d, peer in enumerate(peers):
        remote(ext.at[grp], ext.at[grp], ext_send.at[d], ext_recv.at[d], {"grp": peer}).wait()
        remote(
            gath.at[0, grp], gath.at[0, grp], gath_send.at[0, d], gath_recv.at[0, d], {"grp": peer}
        ).wait()
    prepare(0)

    halo_west.wait()
    halo_east.wait()

    @pl.when(has_south)
    def _():
        halo_south.wait_send()
        halo_north.wait_recv()

    @pl.when(has_north)
    def _():
        halo_north.wait_send()
        halo_south.wait_recv()

    def lon_copies(chunk):
        rows = pl.ds(chunk * 4 + 2, 4)
        to_w = remote(
            field.at[1, rows, pl.ds(2, 2)], field.at[1, rows, pl.ds(18, 2)],
            lon_send.at[0, chunk], lon_recv.at[0, chunk], {"lon": west},
        )
        to_e = remote(
            field.at[1, rows, pl.ds(16, 2)], field.at[1, rows, pl.ds(0, 2)],
            lon_send.at[1, chunk], lon_recv.at[1, chunk], {"lon": east},
        )
        return to_w, to_e

    next_south, next_north = lat_copies(1, lat_send, lat_recv)

    def first_write(j, i, value):
        field[1, j + 2, i + 2] = value

    def first_chunk(n, _):
        chunk = (3 * n) % 4

        def row(r, _):
            advance(0, chunk * 4 + r, first_write)
            return 0

        lax.fori_loop(0, 4, row, 0)
        for copy in lon_copies(chunk):
            copy.start()

        @pl.when(jnp.logical_and(n == 0, has_south))
        def _():
            next_south.start()

        @pl.when(jnp.logical_and(n == 1, has_north))
        def _():
            next_north.start()

        return 0

    lax.fori_loop(0, 4, first_chunk, 0)

    for d, peer in enumerate(peers):
        remote(
            gath.at[1, grp], gath.at[1, grp], gath_send.at[1, d], gath_recv.at[1, d], {"grp": peer}
        ).wait()
    prepare(1)

    @pl.when(has_south)
    def _():
        next_south.wait_send()
        next_north.wait_recv()

    @pl.when(has_north)
    def _():
        next_north.wait_send()
        next_south.wait_recv()

    def second_write(j, i, value):
        done[pl.ds(i * 16 + j, 8, stride=256), :] = value

    def second_chunk(n, _):
        chunk = (3 * n) % 4
        for copy in lon_copies(chunk):
            copy.wait()

        def row(r, _):
            advance(1, chunk * 4 + r, second_write)
            return 0

        lax.fori_loop(0, 4, row, 0)
        return 0

    lax.fori_loop(0, 4, second_chunk, 0)
    to_west.wait_send()

    @pl.when(has_south)
    def _():
        to_south.wait_send()

    result = pltpu.make_async_copy(done, out, out_sem)
    result.start()
    result.wait()


def on_device(tracers, fluxes, limiter_mask, diffusion_inverse):
    f32 = jnp.float32
    dma = pltpu.SemaphoreType.DMA
    out = pl.pallas_call(
        kernel,
        out_shape=jax.ShapeDtypeStruct((2048, LANES), f32),
        in_specs=[pl.BlockSpec(memory_space=pl.ANY)] * 4,
        out_specs=pl.BlockSpec(memory_space=pl.ANY),
        scratch_shapes=[
            pltpu.VMEM((2, 768, 16), f32),
            pltpu.VMEM((2, 8, 96, LANES), f32),
            pltpu.VMEM((3, 8, LANES), f32),
            pltpu.VMEM((8, 8, LANES), f32),
            pltpu.VMEM((2048, LANES), f32),
            pltpu.VMEM((2, 20, 20, 8, LANES), f32),
            pltpu.VMEM((2, 16, 128, 128), f32),
            pltpu.VMEM((2, 16, 256, 256), jnp.bfloat16),
            pltpu.VMEM((POINTS, 16, 16, LANES), f32),
            pltpu.VMEM((3, 17, 24, LANES), f32),
            pltpu.VMEM((2, 16, 16, LANES), jnp.int32),
            pltpu.VMEM((128, 256), jnp.bfloat16),
            pltpu.VMEM((2048, LANES), f32),
            dma((5,)), dma,
            dma((2,)), dma((2,)),
            dma((7,)), dma((7,)),
            dma((2, 7)), dma((2, 7)),
            dma((4,)), dma((4,)),
            dma((2, 4)), dma((2, 4)),
            dma((2,)), dma((2,)),
        ],
        compiler_params=pltpu.CompilerParams(
            collective_id=0, has_side_effects=True, vmem_limit_bytes=40 * 1024 * 1024
        ),
        name="transport",
    )(
        tracers.reshape(2048, LANES), fluxes.reshape(2, 768, 16), limiter_mask, diffusion_inverse
    )
    return out.reshape(8, 16, 16, LANES)


def solution(mesh):
    in_specs = (
        P("grp", "lon", "lat", None),
        P(None, None, "lon", "lat", "grp"),
        P(None, "lon", "lat", None),
        P(None, "lat", None, None),
    )
    out_specs = P("grp", "lon", "lat", None)
    return jax.shard_map(
        on_device, mesh=mesh, in_specs=in_specs, out_specs=out_specs, check_vma=False
    )
```

```python
import functools

import jax
import jax.numpy as jnp
from jax import lax
from jax.experimental import pallas as pl
from jax.experimental.pallas import tpu as pltpu
from jax.sharding import PartitionSpec as P

MESH = pl.DeviceIdType.MESH
LANES = 128
POINTS = 13


def faces(courant, first=None):
    plus, minus = jnp.maximum(courant, 0.0), jnp.minimum(courant, 0.0)
    p, m = plus * (1.0 / 6.0), minus * (1.0 / 6.0)
    a, b, c, d = -p, 5.0 * p + 2.0 * m, 2.0 * p + 5.0 * m, -m
    if first is not None:
        a, b = jnp.where(first, 0.0, a), jnp.where(first, plus, b)
        c, d = jnp.where(first, minus, c), jnp.where(first, 0.0, d)
    return a, b, c, d


def spread(low, high):
    a, b, c, d = low
    e, f, g, h = high
    return a, b - e, c - f, d - g, -h


def block_transpose(blocks, lane):
    blocks = list(blocks)
    for bit in (1, 2, 4):
        odd = (lane // (16 * bit)) % 2 == 1
        for g in range(8):
            if g & bit:
                continue
            low, high = blocks[g], blocks[g + bit]
            blocks[g] = jnp.where(odd, pltpu.roll(high, 16 * bit, 1), low)
            blocks[g + bit] = jnp.where(odd, high, pltpu.roll(low, LANES - 16 * bit, 1))
    return blocks


def kernel(
    tracers, fluxes, limiter, inverse, out,
    shard, gath, near, ext, start, field0, field1, given, weights, coef, courant, lim,
    even_split, odd_split, done, in_sem, out_sem, near_send, near_recv, ext_send, ext_recv, gath_send, gath_recv,
    halo_send, halo_recv, lon_send, lon_recv, lat_send, lat_recv,
):
    groups, lons, lats = lax.axis_size("grp"), lax.axis_size("lon"), lax.axis_size("lat")
    grp, lon, lat = lax.axis_index("grp"), lax.axis_index("lon"), lax.axis_index("lat")
    east, west = lax.rem(lon + 1, lons), lax.rem(lon + lons - 1, lons)
    has_south, has_north = lat > 0, lat < lats - 1
    south, north = lat - 1, lat + 1
    peers = [lax.rem(grp + d, groups) for d in range(1, groups)]
    lane = lax.broadcasted_iota(jnp.int32, (8, LANES), 1)
    sub = lax.broadcasted_iota(jnp.int32, (8, LANES), 0)

    def remote(src, dst, send, recv, where):
        return pltpu.make_async_remote_copy(
            src_ref=src, dst_ref=dst, send_sem=send, recv_sem=recv,
            device_id=where, device_id_type=MESH,
        )

    loads = [
        pltpu.make_async_copy(fluxes.at[0], shard.at[0], in_sem.at[0]),
        pltpu.make_async_copy(tracers, start, in_sem.at[1]),
        pltpu.make_async_copy(fluxes.at[1], shard.at[1], in_sem.at[2]),
        pltpu.make_async_copy(limiter, lim, in_sem.at[3]),
        pltpu.make_async_copy(inverse, given, in_sem.at[4]),
    ]
    for load in loads:
        load.start()

    barrier = pltpu.get_barrier_semaphore()
    for peer in peers:
        pl.semaphore_signal(barrier, inc=1, device_id={"grp": peer}, device_id_type=MESH)
    for side in (east, west):
        pl.semaphore_signal(barrier, inc=1, device_id={"lon": side}, device_id_type=MESH)

    @pl.when(has_south)
    def _():
        pl.semaphore_signal(barrier, inc=1, device_id={"lat": south}, device_id_type=MESH)

    @pl.when(has_north)
    def _():
        pl.semaphore_signal(barrier, inc=1, device_id={"lat": north}, device_id_type=MESH)

    def pack(step):
        def body(c, _):
            for q in range(4):
                base = pl.multiple_of(c * 256 + (q // 2) * 128 + (q % 2) * 8, 8)
                parts = [shard[step, pl.ds(base + 16 * r, 8), :] for r in range(8)]
                rows = pl.ds(pl.multiple_of(c * 32 + q * 8, 8), 8)
                gath[step, grp, rows, :] = jnp.concatenate(parts, axis=1)
            return 0

        lax.fori_loop(0, 3, body, 0)

    def send_gath(step):
        for d, peer in enumerate(peers):
            remote(
                gath.at[step, grp], gath.at[step, grp],
                gath_send.at[step, d], gath_recv.at[step, d], {"grp": peer},
            ).start()

    loads[0].wait()
    pack(0)
    loads[2].wait()
    cols = [shard[s, pl.ds(8 * jb, 8), :] for s in range(2) for jb in range(2)]
    rows = [shard[s, pl.ds(256 + 128 * ib, 8, stride=16), :] for s in range(2) for ib in range(2)]
    near[0] = jnp.concatenate(cols + rows, axis=1)

    pl.semaphore_wait(barrier, groups + 1 + jnp.minimum(lat, 1) + jnp.minimum(lats - 1 - lat, 1))

    to_west = remote(near.at[0], near.at[1], near_send.at[0], near_recv.at[0], {"lon": west})
    to_south = remote(near.at[0], near.at[2], near_send.at[1], near_recv.at[1], {"lat": south})
    to_west.start()

    @pl.when(has_south)
    def _():
        to_south.start()

    send_gath(0)

    loads[1].wait()

    def turn(j, _):
        for i in range(16):
            field0[j + 2, i + 2] = start[pl.ds(i * 16 + j, 8, stride=256), :]
        return 0

    lax.fori_loop(0, 16, turn, 0)

    for field in (field0, field1):
        @pl.when(jnp.logical_not(has_south))
        def _():
            field[0:2] = jnp.zeros((2, 20, 8, LANES), jnp.float32)

        @pl.when(jnp.logical_not(has_north))
        def _():
            field[18:20] = jnp.zeros((2, 20, 8, LANES), jnp.float32)

    halo_west = remote(
        field0.at[pl.ds(2, 16), pl.ds(2, 2)], field0.at[pl.ds(2, 16), pl.ds(18, 2)],
        halo_send.at[0], halo_recv.at[0], {"lon": west},
    )
    halo_east = remote(
        field0.at[pl.ds(2, 16), pl.ds(16, 2)], field0.at[pl.ds(2, 16), pl.ds(0, 2)],
        halo_send.at[1], halo_recv.at[1], {"lon": east},
    )

    def lat_copies(field, send, recv):
        to_s = remote(
            field.at[pl.ds(2, 2), pl.ds(2, 16)], field.at[pl.ds(18, 2), pl.ds(2, 16)],
            send.at[0], recv.at[0], {"lat": south},
        )
        to_n = remote(
            field.at[pl.ds(16, 2), pl.ds(2, 16)], field.at[pl.ds(0, 2), pl.ds(2, 16)],
            send.at[1], recv.at[1], {"lat": north},
        )
        return to_s, to_n

    halo_south, halo_north = lat_copies(field0, halo_send.at[pl.ds(2, 2)], halo_recv.at[pl.ds(2, 2)])
    halo_west.start()
    halo_east.start()

    @pl.when(has_south)
    def _():
        halo_south.start()

    @pl.when(has_north)
    def _():
        halo_north.start()

    to_west.wait_recv()

    @pl.when(has_north)
    def _():
        to_south.wait_recv()
        ext[grp] = jnp.where(lane < 64, near[1], near[2])

    @pl.when(jnp.logical_not(has_north))
    def _():
        ext[grp] = jnp.where(lane < 64, near[1], 0.0)

    for d, peer in enumerate(peers):
        remote(ext.at[grp], ext.at[grp], ext_send.at[d], ext_recv.at[d], {"grp": peer}).start()

    pack(1)
    send_gath(1)

    loads[4].wait()
    for s in range(2):
        def halve(j, _):
            full = given[s, j]
            high = full.astype(jnp.bfloat16)
            low = (full - high.astype(jnp.float32)).astype(jnp.bfloat16)
            for top in (0, 128):
                weights[s, j, top:top + 128, 0:128] = high
                weights[s, j, top:top + 128, 128:256] = low
            return 0

        lax.fori_loop(0, 16, halve, 0)

    loads[3].wait()
    first_row = lat * 16
    last_row = lats * 16

    def prepare(step):
        def unpack(c, _):
            for q in range(4):
                rows = pl.ds(pl.multiple_of(c * 32 + q * 8, 8), 8)
                full = block_transpose([gath[step, g, rows, :] for g in range(8)], lane)
                for r in range(8):
                    courant[c, (q // 2) * 8 + r, 8 * (q % 2):8 * (q % 2) + 8, :] = full[r]
            return 0

        lax.fori_loop(0, 3, unpack, 0)
        edges = block_transpose([ext[g] for g in range(8)], lane)
        for jb in range(2):
            courant[0, 16, 8 * jb:8 * jb + 8, :] = edges[2 * step + jb]
        for ib in range(2):
            values = edges[4 + 2 * step + ib]
            for r in range(8):
                courant[1, 8 * ib + r, 16:17, :] = values[r:r + 1]

        def lat_faces(v, face_row):
            v = jnp.where((face_row == 0) | (face_row == last_row), 0.0, v)
            return faces(v, (face_row == 1) | (face_row == last_row - 1))

        def columns(n, _):
            for jb in range(2):
                here = pl.ds(8 * jb, 8)
                row = first_row + 8 * jb + sub
                western = faces(courant[0, n * 4, here, :])
                for more in range(4):
                    i = n * 4 + more
                    eastern = faces(courant[0, i + 1, here, :])
                    w2, w1, lon0, e1, e2 = spread(western, eastern)
                    western = eastern
                    s2, s1, lat0, n1, n2 = spread(
                        lat_faces(courant[1, i, here, :], row),
                        lat_faces(courant[1, i, pl.ds(8 * jb + 1, 8), :], row + 1),
                    )
                    up = jnp.where(lane == 0, 0.0, courant[2, i, here, :])
                    low = faces(up, (lane == 1) | (lane == LANES - 1) | (lim[step, i, here, :] == 1))
                    high = [pltpu.roll(x, LANES - 1, 1) for x in low]
                    d2, d1, ver0, u1, u2 = spread(low, high)
                    every = (1.0 + lon0 + lat0 + ver0, w2, w1, e1, e2, s2, s1, n1, n2, d2, d1, u1, u2)
                    for point, value in enumerate(every):
                        coef[point, i, here, :] = value
            return 0

        lax.fori_loop(0, 4, columns, 0)

    def stencil(field, j, split):
        mid = [field[j + 2, i] for i in range(20)]
        for pair in range(8):
            new = []
            for i in (2 * pair, 2 * pair + 1):
                c = [jnp.broadcast_to(coef[n, i, pl.ds(j, 1), :], (8, LANES)) for n in range(POINTS)]
                q = mid[i + 2]
                lon_part = c[1] * mid[i] + c[2] * mid[i + 1] + c[3] * mid[i + 3] + c[4] * mid[i + 4]
                lat_part = (
                    c[5] * field[j, i + 2] + c[6] * field[j + 1, i + 2]
                    + c[7] * field[j + 3, i + 2] + c[8] * field[j + 4, i + 2]
                )
                ver_part = (
                    c[9] * pltpu.roll(q, 2, 1) + c[10] * pltpu.roll(q, 1, 1)
                    + c[11] * pltpu.roll(q, LANES - 1, 1) + c[12] * pltpu.roll(q, LANES - 2, 1)
                )
                new.append(c[0] * q + lon_part + (lat_part + ver_part))
            both = jnp.concatenate(new, axis=0)
            high = both.astype(jnp.bfloat16)
            split[16 * pair:16 * pair + 16, 0:128] = high
            split[16 * pair:16 * pair + 16, 128:256] = (both - high.astype(jnp.float32)).astype(jnp.bfloat16)

    def diffuse(step, j, split, write):
        product = jnp.dot(split[...], weights[step, j], preferred_element_type=jnp.float32)
        total = product[:, 0:128] + product[:, 128:256]
        for i in range(16):
            write(j, i, total[8 * i:8 * i + 8])

    def chunk_of(step, n):
        if step == 0:
            return (3 * n) % 4
        late = n // 2
        return late * (n - 2) + (1 - late) * (3 - n)

    def row_of(step, n):
        return chunk_of(step, n // 4) * 4 + n % 4

    def two_rows(step, field, n, write):
        diffuse(step, row_of(step, jnp.maximum(n - 1, 0)), odd_split, write)
        stencil(field, row_of(step, n), even_split)
        diffuse(step, row_of(step, n), even_split, write)
        stencil(field, row_of(step, n + 1), odd_split)

    for d, peer in enumerate(peers):
        remote(ext.at[grp], ext.at[grp], ext_send.at[d], ext_recv.at[d], {"grp": peer}).wait()
        remote(
            gath.at[0, grp], gath.at[0, grp], gath_send.at[0, d], gath_recv.at[0, d], {"grp": peer}
        ).wait()
    prepare(0)

    halo_west.wait()
    halo_east.wait()

    @pl.when(has_south)
    def _():
        halo_south.wait_send()
        halo_north.wait_recv()

    @pl.when(has_north)
    def _():
        halo_north.wait_send()
        halo_south.wait_recv()

    def lon_copies(chunk):
        rows = pl.ds(chunk * 4 + 2, 4)
        to_w = remote(
            field1.at[rows, pl.ds(2, 2)], field1.at[rows, pl.ds(18, 2)],
            lon_send.at[0, chunk], lon_recv.at[0, chunk], {"lon": west},
        )
        to_e = remote(
            field1.at[rows, pl.ds(16, 2)], field1.at[rows, pl.ds(0, 2)],
            lon_send.at[1, chunk], lon_recv.at[1, chunk], {"lon": east},
        )
        return to_w, to_e

    next_south, next_north = lat_copies(field1, lat_send, lat_recv)

    def first_write(j, i, value):
        field1[j + 2, i + 2] = value

    def give(n):
        for copy in lon_copies(chunk_of(0, n)):
            copy.start()

        @pl.when(jnp.logical_and(n == 0, has_south))
        def _():
            next_south.start()

        @pl.when(jnp.logical_and(n == 1, has_north))
        def _():
            next_north.start()

    odd_split[...] = jnp.zeros((128, 256), jnp.bfloat16)

    def first_chunk(n, _):
        two_rows(0, field0, 4 * n, first_write)

        @pl.when(n > 0)
        def _():
            give(n - 1)

        two_rows(0, field0, 4 * n + 2, first_write)
        return 0

    lax.fori_loop(0, 4, first_chunk, 0)
    diffuse(0, row_of(0, 15), odd_split, first_write)
    give(3)

    for d, peer in enumerate(peers):
        remote(
            gath.at[1, grp], gath.at[1, grp], gath_send.at[1, d], gath_recv.at[1, d], {"grp": peer}
        ).wait()
    prepare(1)

    @pl.when(has_south)
    def _():
        next_south.wait_send()
        next_north.wait_recv()

    @pl.when(has_north)
    def _():
        next_north.wait_send()
        next_south.wait_recv()

    results = []
    for half in range(2):
        rows = pl.ds(8 * half, 8)
        here = done.reshape(128, 16, LANES).at[:, rows]
        results.append(pltpu.make_async_copy(here, out.at[:, rows], out_sem.at[half]))

    def second_write(j, i, value):
        done[pl.ds(i * 16 + j, 8, stride=256), :] = value

    def second_chunk(n, _):
        for copy in lon_copies(chunk_of(1, n)):
            copy.wait()
        two_rows(1, field1, 4 * n, second_write)

        @pl.when(n == 2)
        def _():
            results[1].start()

        two_rows(1, field1, 4 * n + 2, second_write)
        return 0

    lax.fori_loop(0, 4, second_chunk, 0)
    diffuse(1, row_of(1, 15), odd_split, second_write)
    results[0].start()
    to_west.wait_send()

    @pl.when(has_south)
    def _():
        to_south.wait_send()

    for result in results:
        result.wait()


def on_device(tracers, fluxes, limiter_mask, diffusion_inverse):
    f32 = jnp.float32
    dma = pltpu.SemaphoreType.DMA
    out = pl.pallas_call(
        kernel,
        out_shape=jax.ShapeDtypeStruct((128, 16, LANES), f32),
        in_specs=[pl.BlockSpec(memory_space=pl.ANY)] * 4,
        out_specs=pl.BlockSpec(memory_space=pl.ANY),
        scratch_shapes=[
            pltpu.VMEM((2, 768, 16), f32),
            pltpu.VMEM((2, 8, 96, LANES), f32),
            pltpu.VMEM((3, 8, LANES), f32),
            pltpu.VMEM((8, 8, LANES), f32),
            pltpu.VMEM((2048, LANES), f32),
            pltpu.VMEM((20, 20, 8, LANES), f32),
            pltpu.VMEM((20, 20, 8, LANES), f32),
            pltpu.VMEM((2, 16, 128, 128), f32),
            pltpu.VMEM((2, 16, 256, 256), jnp.bfloat16),
            pltpu.VMEM((POINTS, 16, 16, LANES), f32),
            pltpu.VMEM((3, 17, 24, LANES), f32),
            pltpu.VMEM((2, 16, 16, LANES), jnp.int32),
            pltpu.VMEM((128, 256), jnp.bfloat16),
            pltpu.VMEM((128, 256), jnp.bfloat16),
            pltpu.VMEM((2048, LANES), f32),
            dma((5,)), dma((2,)),
            dma((2,)), dma((2,)),
            dma((7,)), dma((7,)),
            dma((2, 7)), dma((2, 7)),
            dma((4,)), dma((4,)),
            dma((2, 4)), dma((2, 4)),
            dma((2,)), dma((2,)),
        ],
        compiler_params=pltpu.CompilerParams(
            collective_id=0, has_side_effects=True, vmem_limit_bytes=58 * 1024 * 1024
        ),
        name="transport",
    )(
        tracers.reshape(2048, LANES), fluxes.reshape(2, 768, 16), limiter_mask, diffusion_inverse
    )
    return out.reshape(8, 16, 16, LANES)


def solution(mesh):
    in_specs = (
        P("grp", "lon", "lat", None),
        P(None, None, "lon", "lat", "grp"),
        P(None, "lon", "lat", None),
        P(None, "lat", None, None),
    )
    out_specs = P("grp", "lon", "lat", None)
    return jax.shard_map(
        on_device, mesh=mesh, in_specs=in_specs, out_specs=out_specs, check_vma=False
    )
```

```python
import functools

import jax
import jax.numpy as jnp
from jax import lax
from jax.experimental import pallas as pl
from jax.experimental.pallas import tpu as pltpu
from jax.sharding import PartitionSpec as P

MESH = pl.DeviceIdType.MESH
LANES = 128
POINTS = 13


def faces(courant, first=None):
    plus, minus = jnp.maximum(courant, 0.0), jnp.minimum(courant, 0.0)
    p, m = plus * (1.0 / 6.0), minus * (1.0 / 6.0)
    a, b, c, d = -p, 5.0 * p + 2.0 * m, 2.0 * p + 5.0 * m, -m
    if first is not None:
        a, b = jnp.where(first, 0.0, a), jnp.where(first, plus, b)
        c, d = jnp.where(first, minus, c), jnp.where(first, 0.0, d)
    return a, b, c, d


def spread(low, high):
    a, b, c, d = low
    e, f, g, h = high
    return a, b - e, c - f, d - g, -h


def block_transpose(blocks, lane):
    blocks = list(blocks)
    for bit in (1, 2, 4):
        odd = (lane // (16 * bit)) % 2 == 1
        for g in range(8):
            if g & bit:
                continue
            low, high = blocks[g], blocks[g + bit]
            blocks[g] = jnp.where(odd, pltpu.roll(high, 16 * bit, 1), low)
            blocks[g + bit] = jnp.where(odd, high, pltpu.roll(low, LANES - 16 * bit, 1))
    return blocks


def kernel(
    tracers, fluxes, limiter, inverse, out,
    shard, gath, near, ext, start, field0, field1, given, weights, coef, courant, lim,
    even_split, odd_split, done, in_sem, out_sem, near_send, near_recv, ext_send, ext_recv, gath_send, gath_recv,
    halo_send, halo_recv, lon_send, lon_recv, lat_send, lat_recv,
):
    groups, lons, lats = lax.axis_size("grp"), lax.axis_size("lon"), lax.axis_size("lat")
    grp, lon, lat = lax.axis_index("grp"), lax.axis_index("lon"), lax.axis_index("lat")
    east, west = lax.rem(lon + 1, lons), lax.rem(lon + lons - 1, lons)
    has_south, has_north = lat > 0, lat < lats - 1
    south, north = lat - 1, lat + 1
    peers = [
        lax.rem(grp // 2 + dx, groups // 2) * 2 + lax.rem(grp + dy, 2)
        for dx, dy in ((2, 1), (1, 1), (3, 1), (2, 0), (0, 1), (1, 0), (3, 0))
    ]
    lane = lax.broadcasted_iota(jnp.int32, (8, LANES), 1)
    sub = lax.broadcasted_iota(jnp.int32, (8, LANES), 0)

    def remote(src, dst, send, recv, where):
        return pltpu.make_async_remote_copy(
            src_ref=src, dst_ref=dst, send_sem=send, recv_sem=recv,
            device_id=where, device_id_type=MESH,
        )

    loads = [
        pltpu.make_async_copy(fluxes.at[0], shard.at[0], in_sem.at[0]),
        pltpu.make_async_copy(fluxes.at[1], shard.at[1], in_sem.at[1]),
        pltpu.make_async_copy(tracers, start, in_sem.at[2]),
        pltpu.make_async_copy(limiter, lim, in_sem.at[3]),
        pltpu.make_async_copy(inverse, given, in_sem.at[4]),
    ]
    for load in loads:
        load.start()

    barrier = pltpu.get_barrier_semaphore()
    for peer in peers:
        pl.semaphore_signal(barrier, inc=1, device_id={"grp": peer}, device_id_type=MESH)
    for side in (east, west):
        pl.semaphore_signal(barrier, inc=1, device_id={"lon": side}, device_id_type=MESH)

    @pl.when(has_south)
    def _():
        pl.semaphore_signal(barrier, inc=1, device_id={"lat": south}, device_id_type=MESH)

    @pl.when(has_north)
    def _():
        pl.semaphore_signal(barrier, inc=1, device_id={"lat": north}, device_id_type=MESH)

    def pack(step):
        def body(c, _):
            for q in range(4):
                base = pl.multiple_of(c * 256 + (q // 2) * 128 + (q % 2) * 8, 8)
                parts = [shard[step, pl.ds(base + 16 * r, 8), :] for r in range(8)]
                rows = pl.ds(pl.multiple_of(c * 32 + q * 8, 8), 8)
                gath[step, grp, rows, :] = jnp.concatenate(parts, axis=1)
            return 0

        lax.fori_loop(0, 3, body, 0)

    def send_gath(step):
        for d, peer in enumerate(peers):
            remote(
                gath.at[step, grp], gath.at[step, grp],
                gath_send.at[step, d], gath_recv.at[step, d], {"grp": peer},
            ).start()

    for step in range(2):
        loads[step].wait()
        pack(step)
    cols = [shard[s, pl.ds(8 * jb, 8), :] for s in range(2) for jb in range(2)]
    rows = [shard[s, pl.ds(256 + 128 * ib, 8, stride=16), :] for s in range(2) for ib in range(2)]
    near[0] = jnp.concatenate(cols + rows, axis=1)


    loads[2].wait()

    def turn(j, _):
        for i in range(16):
            field0[j + 2, i + 2] = start[pl.ds(i * 16 + j, 8, stride=256), :]
        return 0

    lax.fori_loop(0, 16, turn, 0)

    for field in (field0, field1):
        @pl.when(jnp.logical_not(has_south))
        def _():
            field[0:2] = jnp.zeros((2, 20, 8, LANES), jnp.float32)

        @pl.when(jnp.logical_not(has_north))
        def _():
            field[18:20] = jnp.zeros((2, 20, 8, LANES), jnp.float32)

    pl.semaphore_wait(barrier, groups + 1 + jnp.minimum(lat, 1) + jnp.minimum(lats - 1 - lat, 1))

    to_west = remote(near.at[0], near.at[1], near_send.at[0], near_recv.at[0], {"lon": west})
    to_south = remote(near.at[0], near.at[2], near_send.at[1], near_recv.at[1], {"lat": south})
    to_west.start()

    @pl.when(has_south)
    def _():
        to_south.start()

    halo_west = remote(
        field0.at[pl.ds(2, 16), pl.ds(2, 2)], field0.at[pl.ds(2, 16), pl.ds(18, 2)],
        halo_send.at[0], halo_recv.at[0], {"lon": west},
    )
    halo_east = remote(
        field0.at[pl.ds(2, 16), pl.ds(16, 2)], field0.at[pl.ds(2, 16), pl.ds(0, 2)],
        halo_send.at[1], halo_recv.at[1], {"lon": east},
    )

    def lat_copies(field, send, recv):
        to_s = remote(
            field.at[pl.ds(2, 2), pl.ds(2, 16)], field.at[pl.ds(18, 2), pl.ds(2, 16)],
            send.at[0], recv.at[0], {"lat": south},
        )
        to_n = remote(
            field.at[pl.ds(16, 2), pl.ds(2, 16)], field.at[pl.ds(0, 2), pl.ds(2, 16)],
            send.at[1], recv.at[1], {"lat": north},
        )
        return to_s, to_n

    halo_south, halo_north = lat_copies(field0, halo_send.at[pl.ds(2, 2)], halo_recv.at[pl.ds(2, 2)])
    halo_west.start()
    halo_east.start()

    @pl.when(has_south)
    def _():
        halo_south.start()

    @pl.when(has_north)
    def _():
        halo_north.start()

    send_gath(0)

    to_west.wait_recv()

    @pl.when(has_north)
    def _():
        to_south.wait_recv()
        ext[grp] = jnp.where(lane < 64, near[1], near[2])

    @pl.when(jnp.logical_not(has_north))
    def _():
        ext[grp] = jnp.where(lane < 64, near[1], 0.0)

    for d, peer in enumerate(peers):
        remote(ext.at[grp], ext.at[grp], ext_send.at[d], ext_recv.at[d], {"grp": peer}).start()


    loads[4].wait()
    for s in range(2):
        def halve(j, _):
            full = given[s, j]
            high = full.astype(jnp.bfloat16)
            low = (full - high.astype(jnp.float32)).astype(jnp.bfloat16)
            for top in (0, 128):
                weights[s, j, top:top + 128, 0:128] = high
                weights[s, j, top:top + 128, 128:256] = low
            return 0

        lax.fori_loop(0, 16, halve, 0)

    loads[3].wait()
    first_row = lat * 16
    last_row = lats * 16

    def prepare(step):
        def unpack(c, _):
            for q in range(4):
                rows = pl.ds(pl.multiple_of(c * 32 + q * 8, 8), 8)
                full = block_transpose([gath[step, g, rows, :] for g in range(8)], lane)
                for r in range(8):
                    courant[c, (q // 2) * 8 + r, 8 * (q % 2):8 * (q % 2) + 8, :] = full[r]
            return 0

        lax.fori_loop(0, 3, unpack, 0)
        edges = block_transpose([ext[g] for g in range(8)], lane)
        for jb in range(2):
            courant[0, 16, 8 * jb:8 * jb + 8, :] = edges[2 * step + jb]
        for ib in range(2):
            values = edges[4 + 2 * step + ib]
            for r in range(8):
                courant[1, 8 * ib + r, 16:17, :] = values[r:r + 1]

        def lat_faces(v, face_row):
            v = jnp.where((face_row == 0) | (face_row == last_row), 0.0, v)
            return faces(v, (face_row == 1) | (face_row == last_row - 1))

        def columns(n, _):
            for jb in range(2):
                here = pl.ds(8 * jb, 8)
                row = first_row + 8 * jb + sub
                western = faces(courant[0, n * 4, here, :])
                for more in range(4):
                    i = n * 4 + more
                    eastern = faces(courant[0, i + 1, here, :])
                    w2, w1, lon0, e1, e2 = spread(western, eastern)
                    western = eastern
                    s2, s1, lat0, n1, n2 = spread(
                        lat_faces(courant[1, i, here, :], row),
                        lat_faces(courant[1, i, pl.ds(8 * jb + 1, 8), :], row + 1),
                    )
                    up = jnp.where(lane == 0, 0.0, courant[2, i, here, :])
                    low = faces(up, (lane == 1) | (lane == LANES - 1) | (lim[step, i, here, :] == 1))
                    high = [pltpu.roll(x, LANES - 1, 1) for x in low]
                    d2, d1, ver0, u1, u2 = spread(low, high)
                    every = (1.0 + lon0 + lat0 + ver0, w2, w1, e1, e2, s2, s1, n1, n2, d2, d1, u1, u2)
                    for point, value in enumerate(every):
                        coef[point, i, here, :] = value
            return 0

        lax.fori_loop(0, 4, columns, 0)

    def stencil(field, j, split):
        mid = [field[j + 2, i] for i in range(20)]
        for pair in range(8):
            new = []
            for i in (2 * pair, 2 * pair + 1):
                c = [jnp.broadcast_to(coef[n, i, pl.ds(j, 1), :], (8, LANES)) for n in range(POINTS)]
                q = mid[i + 2]
                lon_part = c[1] * mid[i] + c[2] * mid[i + 1] + c[3] * mid[i + 3] + c[4] * mid[i + 4]
                lat_part = (
                    c[5] * field[j, i + 2] + c[6] * field[j + 1, i + 2]
                    + c[7] * field[j + 3, i + 2] + c[8] * field[j + 4, i + 2]
                )
                ver_part = (
                    c[9] * pltpu.roll(q, 2, 1) + c[10] * pltpu.roll(q, 1, 1)
                    + c[11] * pltpu.roll(q, LANES - 1, 1) + c[12] * pltpu.roll(q, LANES - 2, 1)
                )
                new.append(c[0] * q + lon_part + (lat_part + ver_part))
            both = jnp.concatenate(new, axis=0)
            high = both.astype(jnp.bfloat16)
            split[16 * pair:16 * pair + 16, 0:128] = high
            split[16 * pair:16 * pair + 16, 128:256] = (both - high.astype(jnp.float32)).astype(jnp.bfloat16)

    def diffuse(step, j, split, write):
        product = jnp.dot(split[...], weights[step, j], preferred_element_type=jnp.float32)
        total = product[:, 0:128] + product[:, 128:256]
        for i in range(16):
            write(j, i, total[8 * i:8 * i + 8])

    def chunk_of(step, n):
        if step == 0:
            return (3 * n) % 4
        late = n // 2
        return late * (n - 2) + (1 - late) * (3 - n)

    def row_of(step, n):
        return chunk_of(step, n // 4) * 4 + n % 4

    def two_rows(step, field, n, write):
        diffuse(step, row_of(step, jnp.maximum(n - 1, 0)), odd_split, write)
        stencil(field, row_of(step, n), even_split)
        diffuse(step, row_of(step, n), even_split, write)
        stencil(field, row_of(step, n + 1), odd_split)

    for d, peer in enumerate(peers):
        remote(
            gath.at[0, grp], gath.at[0, grp], gath_send.at[0, d], gath_recv.at[0, d], {"grp": peer}
        ).wait_send()
    send_gath(1)
    for d, peer in enumerate(peers):
        remote(ext.at[grp], ext.at[grp], ext_send.at[d], ext_recv.at[d], {"grp": peer}).wait()
        remote(
            gath.at[0, grp], gath.at[0, grp], gath_send.at[0, d], gath_recv.at[0, d], {"grp": peer}
        ).wait_recv()
    prepare(0)

    halo_west.wait()
    halo_east.wait()

    @pl.when(has_south)
    def _():
        halo_south.wait_send()
        halo_north.wait_recv()

    @pl.when(has_north)
    def _():
        halo_north.wait_send()
        halo_south.wait_recv()

    def lon_copies(chunk):
        rows = pl.ds(chunk * 4 + 2, 4)
        to_w = remote(
            field1.at[rows, pl.ds(2, 2)], field1.at[rows, pl.ds(18, 2)],
            lon_send.at[0, chunk], lon_recv.at[0, chunk], {"lon": west},
        )
        to_e = remote(
            field1.at[rows, pl.ds(16, 2)], field1.at[rows, pl.ds(0, 2)],
            lon_send.at[1, chunk], lon_recv.at[1, chunk], {"lon": east},
        )
        return to_w, to_e

    next_south, next_north = lat_copies(field1, lat_send, lat_recv)

    def first_write(j, i, value):
        field1[j + 2, i + 2] = value

    def give(n):
        for copy in lon_copies(chunk_of(0, n)):
            copy.start()

        @pl.when(jnp.logical_and(n == 0, has_south))
        def _():
            next_south.start()

        @pl.when(jnp.logical_and(n == 1, has_north))
        def _():
            next_north.start()

    odd_split[...] = jnp.zeros((128, 256), jnp.bfloat16)

    def first_chunk(n, _):
        two_rows(0, field0, 4 * n, first_write)

        @pl.when(n > 0)
        def _():
            give(n - 1)

        two_rows(0, field0, 4 * n + 2, first_write)
        return 0

    lax.fori_loop(0, 4, first_chunk, 0)
    diffuse(0, row_of(0, 15), odd_split, first_write)
    give(3)

    for d, peer in enumerate(peers):
        remote(
            gath.at[1, grp], gath.at[1, grp], gath_send.at[1, d], gath_recv.at[1, d], {"grp": peer}
        ).wait()
    prepare(1)

    @pl.when(has_south)
    def _():
        next_south.wait_send()
        next_north.wait_recv()

    @pl.when(has_north)
    def _():
        next_north.wait_send()
        next_south.wait_recv()

    results = []
    for half in range(2):
        rows = pl.ds(8 * half, 8)
        here = done.reshape(128, 16, LANES).at[:, rows]
        results.append(pltpu.make_async_copy(here, out.at[:, rows], out_sem.at[half]))

    def second_write(j, i, value):
        done[pl.ds(i * 16 + j, 8, stride=256), :] = value

    def second_chunk(n, _):
        for copy in lon_copies(chunk_of(1, n)):
            copy.wait()
        two_rows(1, field1, 4 * n, second_write)

        @pl.when(n == 2)
        def _():
            results[1].start()

        two_rows(1, field1, 4 * n + 2, second_write)
        return 0

    lax.fori_loop(0, 4, second_chunk, 0)
    diffuse(1, row_of(1, 15), odd_split, second_write)
    results[0].start()
    to_west.wait_send()

    @pl.when(has_south)
    def _():
        to_south.wait_send()

    for result in results:
        result.wait()


def on_device(tracers, fluxes, limiter_mask, diffusion_inverse):
    f32 = jnp.float32
    dma = pltpu.SemaphoreType.DMA
    out = pl.pallas_call(
        kernel,
        out_shape=jax.ShapeDtypeStruct((128, 16, LANES), f32),
        in_specs=[pl.BlockSpec(memory_space=pl.ANY)] * 4,
        out_specs=pl.BlockSpec(memory_space=pl.ANY),
        scratch_shapes=[
            pltpu.VMEM((2, 768, 16), f32),
            pltpu.VMEM((2, 8, 96, LANES), f32),
            pltpu.VMEM((3, 8, LANES), f32),
            pltpu.VMEM((8, 8, LANES), f32),
            pltpu.VMEM((2048, LANES), f32),
            pltpu.VMEM((20, 20, 8, LANES), f32),
            pltpu.VMEM((20, 20, 8, LANES), f32),
            pltpu.VMEM((2, 16, 128, 128), f32),
            pltpu.VMEM((2, 16, 256, 256), jnp.bfloat16),
            pltpu.VMEM((POINTS, 16, 16, LANES), f32),
            pltpu.VMEM((3, 17, 24, LANES), f32),
            pltpu.VMEM((2, 16, 16, LANES), jnp.int32),
            pltpu.VMEM((128, 256), jnp.bfloat16),
            pltpu.VMEM((128, 256), jnp.bfloat16),
            pltpu.VMEM((2048, LANES), f32),
            dma((5,)), dma((2,)),
            dma((2,)), dma((2,)),
            dma((7,)), dma((7,)),
            dma((2, 7)), dma((2, 7)),
            dma((4,)), dma((4,)),
            dma((2, 4)), dma((2, 4)),
            dma((2,)), dma((2,)),
        ],
        compiler_params=pltpu.CompilerParams(
            collective_id=0, has_side_effects=True, vmem_limit_bytes=58 * 1024 * 1024
        ),
        name="transport",
    )(
        tracers.reshape(2048, LANES), fluxes.reshape(2, 768, 16), limiter_mask, diffusion_inverse
    )
    return out.reshape(8, 16, 16, LANES)


def solution(mesh):
    in_specs = (
        P("grp", "lon", "lat", None),
        P(None, None, "lon", "lat", "grp"),
        P(None, "lon", "lat", None),
        P(None, "lat", None, None),
    )
    out_specs = P("grp", "lon", "lat", None)
    return jax.shard_map(
        on_device, mesh=mesh, in_specs=in_specs, out_specs=out_specs, check_vma=False
    )
```

```python
import functools

import jax
import jax.numpy as jnp
from jax import lax
from jax.experimental import pallas as pl
from jax.experimental.pallas import tpu as pltpu
from jax.sharding import PartitionSpec as P

MESH = pl.DeviceIdType.MESH
LANES = 128
POINTS = 13


def faces(courant, first=None):
    plus, minus = jnp.maximum(courant, 0.0), jnp.minimum(courant, 0.0)
    p, m = plus * (1.0 / 6.0), minus * (1.0 / 6.0)
    a, b, c, d = -p, 5.0 * p + 2.0 * m, 2.0 * p + 5.0 * m, -m
    if first is not None:
        a, b = jnp.where(first, 0.0, a), jnp.where(first, plus, b)
        c, d = jnp.where(first, minus, c), jnp.where(first, 0.0, d)
    return a, b, c, d


def spread(low, high):
    a, b, c, d = low
    e, f, g, h = high
    return a, b - e, c - f, d - g, -h


def gathered(blocks, lane):
    blocks = [pltpu.roll(block, 16 * g, 1) if g else block for g, block in enumerate(blocks)]
    odd = [(lane // (16 * bit)) % 2 == 1 for bit in (1, 2, 4)]
    full = []
    for r in range(8):
        parts = [blocks[(b - r) % 8] for b in range(8)]
        for mask in odd:
            parts = [jnp.where(mask, parts[n + 1], parts[n]) for n in range(0, len(parts), 2)]
        full.append(pltpu.roll(parts[0], LANES - 16 * r, 1) if r else parts[0])
    return full


def kernel(
    tracers, fluxes, limiter, inverse, out,
    shard, gath, near, ext, start, field0, field1, given, weights, coef, courant, lim,
    even_split, odd_split, done, in_sem, out_sem, near_send, near_recv, ext_send, ext_recv, gath_send, gath_recv,
    halo_send, halo_recv, lon_send, lon_recv, lat_send, lat_recv,
):
    groups, lons, lats = lax.axis_size("grp"), lax.axis_size("lon"), lax.axis_size("lat")
    grp, lon, lat = lax.axis_index("grp"), lax.axis_index("lon"), lax.axis_index("lat")
    east, west = lax.rem(lon + 1, lons), lax.rem(lon + lons - 1, lons)
    has_south, has_north = lat > 0, lat < lats - 1
    south, north = lat - 1, lat + 1
    peers = [
        lax.rem(grp // 2 + dx, groups // 2) * 2 + lax.rem(grp + dy, 2)
        for dx, dy in ((2, 1), (1, 1), (3, 1), (2, 0), (0, 1), (1, 0), (3, 0))
    ]
    lane = lax.broadcasted_iota(jnp.int32, (8, LANES), 1)
    sub = lax.broadcasted_iota(jnp.int32, (8, LANES), 0)

    def remote(src, dst, send, recv, where):
        return pltpu.make_async_remote_copy(
            src_ref=src, dst_ref=dst, send_sem=send, recv_sem=recv,
            device_id=where, device_id_type=MESH,
        )

    loads = [
        pltpu.make_async_copy(fluxes.at[0], shard.at[0], in_sem.at[0]),
        pltpu.make_async_copy(fluxes.at[1], shard.at[1], in_sem.at[1]),
        pltpu.make_async_copy(tracers, start, in_sem.at[2]),
        pltpu.make_async_copy(limiter, lim, in_sem.at[3]),
        pltpu.make_async_copy(inverse, given, in_sem.at[4]),
    ]
    for load in loads:
        load.start()

    barrier = pltpu.get_barrier_semaphore()
    for peer in peers:
        pl.semaphore_signal(barrier, inc=1, device_id={"grp": peer}, device_id_type=MESH)
    for side in (east, west):
        pl.semaphore_signal(barrier, inc=1, device_id={"lon": side}, device_id_type=MESH)

    @pl.when(has_south)
    def _():
        pl.semaphore_signal(barrier, inc=1, device_id={"lat": south}, device_id_type=MESH)

    @pl.when(has_north)
    def _():
        pl.semaphore_signal(barrier, inc=1, device_id={"lat": north}, device_id_type=MESH)

    def pack(step):
        def body(c, _):
            for q in range(4):
                base = pl.multiple_of(c * 256 + (q // 2) * 128 + (q % 2) * 8, 8)
                parts = [shard[step, pl.ds(base + 16 * r, 8), :] for r in range(8)]
                rows = pl.ds(pl.multiple_of(c * 32 + q * 8, 8), 8)
                gath[step, grp, rows, :] = jnp.concatenate(parts, axis=1)
            return 0

        lax.fori_loop(0, 3, body, 0)

    def send_gath(step):
        for d, peer in enumerate(peers):
            remote(
                gath.at[step, grp], gath.at[step, grp],
                gath_send.at[step, d], gath_recv.at[step, d], {"grp": peer},
            ).start()

    for step in range(2):
        loads[step].wait()
        pack(step)
    cols = [shard[s, pl.ds(8 * jb, 8), :] for s in range(2) for jb in range(2)]
    rows = [shard[s, pl.ds(256 + 128 * ib, 8, stride=16), :] for s in range(2) for ib in range(2)]
    near[0] = jnp.concatenate(cols + rows, axis=1)


    loads[2].wait()

    def turn(j, _):
        for i in range(16):
            field0[j + 2, i + 2] = start[pl.ds(i * 16 + j, 8, stride=256), :]
        return 0

    lax.fori_loop(0, 16, turn, 0)

    for field in (field0, field1):
        @pl.when(jnp.logical_not(has_south))
        def _():
            field[0:2] = jnp.zeros((2, 20, 8, LANES), jnp.float32)

        @pl.when(jnp.logical_not(has_north))
        def _():
            field[18:20] = jnp.zeros((2, 20, 8, LANES), jnp.float32)

    pl.semaphore_wait(barrier, groups + 1 + jnp.minimum(lat, 1) + jnp.minimum(lats - 1 - lat, 1))

    to_west = remote(near.at[0], near.at[1], near_send.at[0], near_recv.at[0], {"lon": west})
    to_south = remote(near.at[0], near.at[2], near_send.at[1], near_recv.at[1], {"lat": south})
    to_west.start()

    @pl.when(has_south)
    def _():
        to_south.start()

    def lon_copies(step, chunk):
        field, rows = (field0, field1)[step], pl.ds(chunk * 4 + 2, 4)
        to_w = remote(
            field.at[rows, pl.ds(2, 2)], field.at[rows, pl.ds(18, 2)],
            lon_send.at[step, 0, chunk], lon_recv.at[step, 0, chunk], {"lon": west},
        )
        to_e = remote(
            field.at[rows, pl.ds(16, 2)], field.at[rows, pl.ds(0, 2)],
            lon_send.at[step, 1, chunk], lon_recv.at[step, 1, chunk], {"lon": east},
        )
        return to_w, to_e

    def lat_copies(field, send, recv):
        to_s = remote(
            field.at[pl.ds(2, 2), pl.ds(2, 16)], field.at[pl.ds(18, 2), pl.ds(2, 16)],
            send.at[0], recv.at[0], {"lat": south},
        )
        to_n = remote(
            field.at[pl.ds(16, 2), pl.ds(2, 16)], field.at[pl.ds(0, 2), pl.ds(2, 16)],
            send.at[1], recv.at[1], {"lat": north},
        )
        return to_s, to_n

    halo_south, halo_north = lat_copies(field0, halo_send, halo_recv)
    for copy in lon_copies(0, 2):
        copy.start()
    for copy in lon_copies(0, 1):
        copy.start()

    @pl.when(has_south)
    def _():
        halo_south.start()

    @pl.when(has_north)
    def _():
        halo_north.start()

    for chunk in (0, 3):
        for copy in lon_copies(0, chunk):
            copy.start()

    send_gath(0)

    to_west.wait_recv()

    @pl.when(has_north)
    def _():
        to_south.wait_recv()
        ext[grp] = jnp.where(lane < 64, near[1], near[2])

    @pl.when(jnp.logical_not(has_north))
    def _():
        ext[grp] = jnp.where(lane < 64, near[1], 0.0)

    for d, peer in enumerate(peers):
        remote(ext.at[grp], ext.at[grp], ext_send.at[d], ext_recv.at[d], {"grp": peer}).start()


    loads[4].wait()
    for s in range(2):
        def halve(j, _):
            full = given[s, j]
            high = full.astype(jnp.bfloat16)
            low = (full - high.astype(jnp.float32)).astype(jnp.bfloat16)
            for top in (0, 128):
                weights[s, j, top:top + 128, 0:128] = high
                weights[s, j, top:top + 128, 128:256] = low
            return 0

        lax.fori_loop(0, 16, halve, 0)

    loads[3].wait()
    first_row = lat * 16
    last_row = lats * 16

    def prepare(step):
        def unpack(c, _):
            for q in range(4):
                rows = pl.ds(pl.multiple_of(c * 32 + q * 8, 8), 8)
                full = gathered([gath[step, g, rows, :] for g in range(8)], lane)
                for r in range(8):
                    courant[c, (q // 2) * 8 + r, 8 * (q % 2):8 * (q % 2) + 8, :] = full[r]
            return 0

        lax.fori_loop(0, 3, unpack, 0)
        edges = gathered([ext[g] for g in range(8)], lane)
        for jb in range(2):
            courant[0, 16, 8 * jb:8 * jb + 8, :] = edges[2 * step + jb]
        for ib in range(2):
            values = edges[4 + 2 * step + ib]
            for r in range(8):
                courant[1, 8 * ib + r, 16:17, :] = values[r:r + 1]

        def lat_faces(v, face_row):
            v = jnp.where((face_row == 0) | (face_row == last_row), 0.0, v)
            return faces(v, (face_row == 1) | (face_row == last_row - 1))

        def columns(n, _):
            for jb in range(2):
                here = pl.ds(8 * jb, 8)
                row = first_row + 8 * jb + sub
                western = faces(courant[0, n * 4, here, :])
                for more in range(4):
                    i = n * 4 + more
                    eastern = faces(courant[0, i + 1, here, :])
                    w2, w1, lon0, e1, e2 = spread(western, eastern)
                    western = eastern
                    s2, s1, lat0, n1, n2 = spread(
                        lat_faces(courant[1, i, here, :], row),
                        lat_faces(courant[1, i, pl.ds(8 * jb + 1, 8), :], row + 1),
                    )
                    up = jnp.where(lane == 0, 0.0, courant[2, i, here, :])
                    d2, b, c, d = faces(up, (lane == 1) | (lane == LANES - 1) | (lim[step, i, here, :] == 1))
                    d1 = b - pltpu.roll(d2, LANES - 1, 1)
                    ver0 = c - pltpu.roll(b, LANES - 1, 1)
                    u1 = pltpu.roll(d, 2, 1) - pltpu.roll(c, 1, 1)
                    u2 = -pltpu.roll(d, 1, 1)
                    every = (1.0 + lon0 + lat0 + ver0, w2, w1, e1, e2, s2, s1, n1, n2, d2, d1, u1, u2)
                    for point, value in enumerate(every):
                        coef[point, i, here, :] = value
            return 0

        lax.fori_loop(0, 4, columns, 0)

    def stencil(field, j, split):
        mid = [field[j + 2, i] for i in range(20)]
        for pair in range(8):
            new = []
            for i in (2 * pair, 2 * pair + 1):
                c = [jnp.broadcast_to(coef[n, i, pl.ds(j, 1), :], (8, LANES)) for n in range(POINTS)]
                q = mid[i + 2]
                lon_part = c[1] * mid[i] + c[2] * mid[i + 1] + c[3] * mid[i + 3] + c[4] * mid[i + 4]
                lat_part = (
                    c[5] * field[j, i + 2] + c[6] * field[j + 1, i + 2]
                    + c[7] * field[j + 3, i + 2] + c[8] * field[j + 4, i + 2]
                )
                below = pltpu.roll(q, 1, 1)
                ver_part = (
                    c[9] * pltpu.roll(q, 2, 1) + c[10] * below
                    + pltpu.roll(c[11] * below + c[12] * q, LANES - 2, 1)
                )
                new.append(c[0] * q + lon_part + (lat_part + ver_part))
            both = jnp.concatenate(new, axis=0)
            high = both.astype(jnp.bfloat16)
            split[16 * pair:16 * pair + 16, 0:128] = high
            split[16 * pair:16 * pair + 16, 128:256] = (both - high.astype(jnp.float32)).astype(jnp.bfloat16)

    def diffuse(step, j, split, write):
        product = jnp.dot(split[...], weights[step, j], preferred_element_type=jnp.float32)
        total = product[:, 0:128] + product[:, 128:256]
        for i in range(16):
            write(j, i, total[8 * i:8 * i + 8])

    def chunk_of(n):
        return 2 - n + 4 * (n // 3)

    def row_of(n):
        return chunk_of(n // 4) * 4 + n % 4

    def two_rows(step, field, n, write):
        diffuse(step, row_of(jnp.maximum(n - 1, 0)), odd_split, write)
        stencil(field, row_of(n), even_split)
        diffuse(step, row_of(n), even_split, write)
        stencil(field, row_of(n + 1), odd_split)

    for d, peer in enumerate(peers):
        remote(
            gath.at[0, grp], gath.at[0, grp], gath_send.at[0, d], gath_recv.at[0, d], {"grp": peer}
        ).wait_send()
    send_gath(1)
    for d, peer in enumerate(peers):
        remote(ext.at[grp], ext.at[grp], ext_send.at[d], ext_recv.at[d], {"grp": peer}).wait()
        remote(
            gath.at[0, grp], gath.at[0, grp], gath_send.at[0, d], gath_recv.at[0, d], {"grp": peer}
        ).wait_recv()
    prepare(0)

    next_south, next_north = lat_copies(field1, lat_send, lat_recv)

    def first_write(j, i, value):
        field1[j + 2, i + 2] = value

    def take(step, n, to_s, to_n):
        for copy in lon_copies(step, chunk_of(n)):
            copy.wait()

        @pl.when(jnp.logical_and(n == 2, has_south))
        def _():
            to_n.wait_recv()

        @pl.when(jnp.logical_and(n == 3, has_north))
        def _():
            to_s.wait_recv()

    def give(n):
        for copy in lon_copies(1, chunk_of(n)):
            copy.start()

        @pl.when(jnp.logical_and(n == 2, has_south))
        def _():
            next_south.start()

        @pl.when(jnp.logical_and(n == 3, has_north))
        def _():
            next_north.start()

    odd_split[...] = jnp.zeros((128, 256), jnp.bfloat16)

    def first_chunk(n, _):
        take(0, n, halo_south, halo_north)
        two_rows(0, field0, 4 * n, first_write)

        @pl.when(n > 0)
        def _():
            give(n - 1)

        two_rows(0, field0, 4 * n + 2, first_write)
        return 0

    lax.fori_loop(0, 4, first_chunk, 0)
    diffuse(0, row_of(15), odd_split, first_write)
    give(3)

    for d, peer in enumerate(peers):
        remote(
            gath.at[1, grp], gath.at[1, grp], gath_send.at[1, d], gath_recv.at[1, d], {"grp": peer}
        ).wait()
    prepare(1)

    results = []
    for half in range(2):
        rows = pl.ds(8 * half, 8)
        here = done.reshape(128, 16, LANES).at[:, rows]
        results.append(pltpu.make_async_copy(here, out.at[:, rows], out_sem.at[half]))

    def second_write(j, i, value):
        done[pl.ds(i * 16 + j, 8, stride=256), :] = value

    def second_chunk(n, _):
        take(1, n, next_south, next_north)
        two_rows(1, field1, 4 * n, second_write)

        @pl.when(n == 3)
        def _():
            results[0].start()

        two_rows(1, field1, 4 * n + 2, second_write)
        return 0

    lax.fori_loop(0, 4, second_chunk, 0)
    diffuse(1, row_of(15), odd_split, second_write)
    results[1].start()
    to_west.wait_send()

    @pl.when(has_south)
    def _():
        to_south.wait_send()
        halo_south.wait_send()
        next_south.wait_send()

    @pl.when(has_north)
    def _():
        halo_north.wait_send()
        next_north.wait_send()

    for result in results:
        result.wait()


def on_device(tracers, fluxes, limiter_mask, diffusion_inverse):
    f32 = jnp.float32
    dma = pltpu.SemaphoreType.DMA
    out = pl.pallas_call(
        kernel,
        out_shape=jax.ShapeDtypeStruct((128, 16, LANES), f32),
        in_specs=[pl.BlockSpec(memory_space=pl.ANY)] * 4,
        out_specs=pl.BlockSpec(memory_space=pl.ANY),
        scratch_shapes=[
            pltpu.VMEM((2, 768, 16), f32),
            pltpu.VMEM((2, 8, 96, LANES), f32),
            pltpu.VMEM((3, 8, LANES), f32),
            pltpu.VMEM((8, 8, LANES), f32),
            pltpu.VMEM((2048, LANES), f32),
            pltpu.VMEM((20, 20, 8, LANES), f32),
            pltpu.VMEM((20, 20, 8, LANES), f32),
            pltpu.VMEM((2, 16, 128, 128), f32),
            pltpu.VMEM((2, 16, 256, 256), jnp.bfloat16),
            pltpu.VMEM((POINTS, 16, 16, LANES), f32),
            pltpu.VMEM((3, 17, 24, LANES), f32),
            pltpu.VMEM((2, 16, 16, LANES), jnp.int32),
            pltpu.VMEM((128, 256), jnp.bfloat16),
            pltpu.VMEM((128, 256), jnp.bfloat16),
            pltpu.VMEM((2048, LANES), f32),
            dma((5,)), dma((2,)),
            dma((2,)), dma((2,)),
            dma((7,)), dma((7,)),
            dma((2, 7)), dma((2, 7)),
            dma((2,)), dma((2,)),
            dma((2, 2, 4)), dma((2, 2, 4)),
            dma((2,)), dma((2,)),
        ],
        compiler_params=pltpu.CompilerParams(
            collective_id=0, has_side_effects=True, vmem_limit_bytes=58 * 1024 * 1024
        ),
        name="transport",
    )(
        tracers.reshape(2048, LANES), fluxes.reshape(2, 768, 16), limiter_mask, diffusion_inverse
    )
    return out.reshape(8, 16, 16, LANES)


def solution(mesh):
    in_specs = (
        P("grp", "lon", "lat", None),
        P(None, None, "lon", "lat", "grp"),
        P(None, "lon", "lat", None),
        P(None, "lat", None, None),
    )
    out_specs = P("grp", "lon", "lat", None)
    return jax.shard_map(
        on_device, mesh=mesh, in_specs=in_specs, out_specs=out_specs, check_vma=False
    )
```
